32 devices in a mesh: row: 4 (over z), col: 8 (over y, x, core).
Axes of the slice: x: 2, y: 2, z: 4, core: 2. Of those that a mesh axis runs over, the one named last changes fastest.
Arguments:
- amplitudes: float32 [1024, 20480], P('col', 'row'), may hold values from -6 to 6
- integrals: float32 [20480, 20480], P('row', 'col'), may hold values from -0.0390625 to 0.0390625
- occ_energy: float32 [64], replicated, may hold values from -1.5 to -0.25
- vir_energy: float32 [256], replicated, may hold values from 0.25 to 1.5
- occ_first: int32 [1024], P('row'), may hold values from 0 to 63
- occ_second: int32 [1024], P('row'), may hold values from 0 to 63
- vir_first: int32 [20480], P('col'), may hold values from 0 to 255
- vir_second: int32 [20480], P('col'), may hold values from 0 to 255
Outputs:
- update: float32 [1024, 20480], P('row', 'col')
The draws below stay inside these ranges and needn't reach their ends.
All inputs are finite; a program needn't handle non-finite values.
Results may differ from the reference program's by a relative error of at most 0.00007.
Values sent between devices are 32-bit elements; how exact they have to be, the bound alone decides.
No kernel may reach another device: no remote copies, remote signals or barrier semaphores. Data moves between devices by JAX's collectives and lax.ppermute only.
A program may use at most 128 MiB of HBM per device.

```python
import jax
import jax.numpy as jnp
from jax import lax

NV = 20480
OPAIRS = 1024
NOCC = 64
NVIR = 256


def place_ends(entries, stream_key, smallest, top_value):
    shape = entries.shape
    index_at = [jax.random.randint(jax.random.fold_in(stream_key, axis), (), 0, shape[axis]) for axis in range(len(shape))]
    entries = entries.at[tuple(index_at)].set(smallest)
    longest = shape.index(max(shape))
    index_at[longest] = (index_at[longest] + 1) % shape[longest]
    return entries.at[tuple(index_at)].set(top_value)


def level_of(rng, shape, shards, least, top_value):
    level, own = 1.0, jax.random.fold_in(rng, 6)
    for dim, parts in shards:
        draws = jnp.exp(jax.random.uniform(jax.random.fold_in(own, dim), (parts,), jnp.float32, least / len(shards), top_value / len(shards)))
        level = level * jnp.repeat(draws, shape[dim] // parts).reshape([-1 if axis == dim else 1 for axis in range(len(shape))])
    return level


def normal_values(stream_key, shape, scale, reach, split=(), dtype=jnp.bfloat16):
    loudness = level_of(stream_key, shape, split, -0.22, 0.18) if split else 1.0
    array = jax.random.normal(stream_key, shape, jnp.float32) * scale * loudness
    return jnp.minimum(jnp.maximum(array, -reach), reach).astype(dtype)


def setup_inputs(seed: int = 0) -> dict:
    splits = jax.random.split(jax.random.key(seed), 9)
    return {
        "amplitudes": normal_values(splits[0], (OPAIRS, NV), 1.0, 6.0, ((0, 8), (1, 4)), jnp.float32),
        "integrals": normal_values(splits[1], (NV, NV), NV ** -0.5, 0.0390625, ((0, 4), (1, 8)), jnp.float32),
        "occ_energy": jnp.clip(jax.random.uniform(splits[2], (NOCC,), jnp.float32, -1.5, -0.25), -1.5, -0.25),
        "vir_energy": jnp.clip(jax.random.uniform(splits[3], (NVIR,), jnp.float32, 0.25, 1.5), 0.25, 1.5),
        "occ_first": place_ends(jax.random.randint(splits[4], (OPAIRS,), 0, NOCC), jax.random.fold_in(splits[4], 1), 0, NOCC - 1).astype(jnp.int32),
        "occ_second": place_ends(jax.random.randint(splits[5], (OPAIRS,), 0, NOCC), jax.random.fold_in(splits[5], 1), 0, NOCC - 1).astype(jnp.int32),
        "vir_first": place_ends(jax.random.randint(splits[6], (NV,), 0, NVIR), jax.random.fold_in(splits[6], 1), 0, NVIR - 1).astype(jnp.int32),
        "vir_second": place_ends(jax.random.randint(splits[7], (NV,), 0, NVIR), jax.random.fold_in(splits[7], 1), 0, NVIR - 1).astype(jnp.int32),
    }


def reference(amplitudes, integrals, occ_energy, vir_energy, occ_first, occ_second, vir_first, vir_second):
    ladder = jnp.dot(amplitudes, integrals, preferred_element_type=jnp.float32, precision=lax.Precision.HIGHEST)
    occ_sum = occ_energy[occ_first] + occ_energy[occ_second]
    vir_sum = vir_energy[vir_first] + vir_energy[vir_second]
    denom = vir_sum[None, :] - occ_sum[:, None]
    return ladder / denom
```

```python
import functools

import jax
import jax.numpy as jnp
from jax import lax
from jax.experimental import pallas as pl
from jax.experimental.pallas import tpu as pltpu
from jax.sharding import PartitionSpec as P

PLAN = ((1, (1, 1)), (1, (1,)), (1, (1,)), (1, (1, 1)))
TILE_BYTES = 5500000


def lookup(table, index):
    positions = jnp.arange(table.shape[0], dtype=jnp.int32)
    picked = jnp.where(index[:, None] == positions[None, :], table[None, :], jnp.float32(0.0))
    return jnp.sum(picked, axis=1)


def halves(values):
    high = values.astype(jnp.bfloat16)
    return high, (values - high.astype(jnp.float32)).astype(jnp.bfloat16)


def product_kernel(m, sources, cuts, place_ref, *refs):
    a_refs, b_ref = refs[:sources], refs[sources]
    out_refs, stacked = refs[sources + 1 : -1], refs[-1]
    rows = stacked.shape[0] // 2

    @pl.when(pl.program_id(0) == 0)
    def _():
        q = 0
        for a_ref in a_refs:
            for at in range(0, a_ref.shape[0], m):
                high, low = halves(a_ref[at : at + m, :])
                start = pl.multiple_of(place_ref[q] * m, m)
                stacked[pl.ds(start, m), :] = high
                stacked[pl.ds(rows + start, m), :] = low
                q += 1

    b_high, b_low = halves(b_ref[...])
    both = jnp.dot(stacked[...], b_high, preferred_element_type=jnp.float32)
    total = both[:rows] + (both[rows:] + jnp.dot(stacked[:rows, :], b_low, preferred_element_type=jnp.float32))
    for out_ref, (first, last) in zip(out_refs, cuts):
        out_ref[...] = total[first:last]


def column_tile(depth, columns, offset):
    best = 128
    for tile in range(128, columns + 1, 128):
        if columns % tile == 0 and offset % tile == 0 and depth * tile * 4 <= TILE_BYTES:
            best = tile
    return best


def product(place, sources, m, integrals, offset, columns, cuts):
    depth = integrals.shape[0]
    rows = m * place.shape[0]
    tile = column_tile(depth, columns, offset)
    return pl.pallas_call(
        functools.partial(product_kernel, m, len(sources), cuts),
        grid=(columns // tile,),
        in_specs=[pl.BlockSpec(memory_space=pltpu.SMEM)]
        + [pl.BlockSpec(source.shape, lambda j: (0, 0), pipeline_mode=pl.Buffered(1)) for source in sources]
        + [pl.BlockSpec((depth, tile), lambda j: (0, j + offset // tile))],
        out_specs=[pl.BlockSpec((last - first, tile), lambda j: (0, j)) for first, last in cuts],
        out_shape=[jax.ShapeDtypeStruct((last - first, columns), jnp.float32) for first, last in cuts],
        scratch_shapes=[pltpu.VMEM((2 * rows, depth), jnp.bfloat16)],
        compiler_params=pltpu.CompilerParams(vmem_limit_bytes=58 * 2**20),
        cost_estimate=pl.CostEstimate(
            flops=6 * rows * depth * columns, bytes_accessed=4 * (depth * columns + rows * (depth + columns)), transcendentals=0
        ),
        name="ladder_product",
    )(place, *sources, integrals)


def across(block, axis, bits, size):
    return lax.ppermute(block, axis, [(i, i ^ bits) for i in range(size)])


def row_parts(own):
    if own % 16:
        return [(0, own, (1,))]
    total = sum(share for share, _ in PLAN)
    out, at, so_far = [], 0, 0
    for share, pieces in PLAN:
        so_far += share
        end = own * so_far // total // 16 * 16
        if end > at:
            out.append((at, end, pieces))
            at = end
    return out


def column_pieces(columns, pieces):
    out, at, so_far = [], 0, 0
    for share in pieces:
        so_far += share
        end = columns * so_far // sum(pieces) // 256 * 256 if so_far < sum(pieces) else columns
        if end > at:
            out.append((at, end - at))
            at = end
    return out


def plain(amplitudes, integrals):
    rows = jnp.dot(
        lax.all_gather(amplitudes, "col", axis=0, tiled=True),
        integrals,
        preferred_element_type=jnp.float32,
        precision=lax.Precision.HIGHEST,
    )
    return lax.psum_scatter(rows, "row", scatter_dimension=0, tiled=True)


class Steps:
    def __init__(self):
        self.held, self.due = {}, {}

    def post(self, key, value, step):
        self.held[key] = value
        self.due.setdefault(step, []).append(key)

    def settle(self, step, value):
        keys = self.due.pop(step, [])
        value, held = lax.optimization_barrier((value, [self.held[key] for key in keys]))
        self.held.update(zip(keys, held))
        return value


def per_device(
    size, col_size, amplitudes, integrals, occ_energy, vir_energy, occ_first, occ_second, vir_first, vir_second
):
    own, columns = amplitudes.shape[0], integrals.shape[1]
    if size & (size - 1) or col_size & (col_size - 1) or col_size % size or columns % 128 or own % 8:
        occ_sum = lookup(occ_energy, occ_first) + lookup(occ_energy, occ_second)
        vir_sum = lookup(vir_energy, vir_first) + lookup(vir_energy, vir_second)
        return plain(amplitudes, integrals) / (vir_sum[None, :] - occ_sum[:, None])
    group = col_size // size
    rounds = size.bit_length() - 1
    order = lax.axis_index("col") ^ jnp.arange(col_size, dtype=jnp.int32)
    differs, owner = lax.axis_index("row") ^ (order // group), 0
    for bit in range(rounds):
        owner = owner * 2 + (differs >> bit) % 2
    place = owner * group + order % group

    parts = row_parts(own)
    todo = []
    for number, (first, last, pieces) in enumerate(parts):
        pieces = column_pieces(columns, pieces)
        for piece, (offset, width) in enumerate(pieces):
            todo.append((number, piece, len(pieces), first, last, offset, width))
    count = len(todo)
    steps = Steps()
    held = steps.held
    evens = list(range(0, col_size, 2))

    def gather(number, wanted, due):
        for q in wanted:
            source, bits = (0, q) if q % 2 == 0 else (q - 1, 1)
            steps.post((number, q), across(held[number, source], "col", bits, col_size), due)

    def send(p, turn):
        _, _, _, first, last, _, _ = todo[p]
        block = group * (last - first)
        half = size // 2**turn // 2 * block
        if turn == 0:
            return across(made[p][1], "row", 1, size)
        values = held["sum", p, turn - 1][half:]
        kept = made[p][0][half : 2 * half]
        for earlier in range(turn - 1):
            kept = kept + held["sum", p, earlier][half : 2 * half]
        return across(values + kept, "row", 2**turn, size)

    def write(update, p):
        _, _, _, first, last, offset, width = todo[p]
        block = group * (last - first)
        ladder = made[p][0][:block]
        for turn in range(rounds):
            ladder = ladder + held["sum", p, turn][:block]
        denom = vir_sum[None, None, offset : offset + width] - occ_sum[:, first:last, None]
        written.add(p)
        return lax.dynamic_update_slice(update, ladder.reshape(group, last - first, width) / denom, (0, first, offset))

    made, written = {}, set()
    held[0, 0] = amplitudes[parts[0][0] : parts[0][1]]
    gather(0, evens[1:], 0)
    gather(0, [q + 1 for q in evens], 0)
    terms_at = min(1, count - 1)
    for step in range(count + 1):
        if step == terms_at:
            steps.post("terms", (vir_first, vir_second, occ_first, occ_second), step)
        place = steps.settle(step, place)
        if step == terms_at:
            vir_first, vir_second, occ_first, occ_second = held["terms"]
            occ_sum = (lookup(occ_energy, occ_first) + lookup(occ_energy, occ_second)).reshape(group, own)
            vir_sum = lookup(vir_energy, vir_first) + lookup(vir_energy, vir_second)
            steps.post("denominators", (occ_sum, vir_sum, jnp.zeros((group, own, columns), jnp.float32)), step + 1)
        if step > terms_at:
            occ_sum, vir_sum, update = held["denominators"]
        if step == count:
            break
        number, piece, pieces, first, last, offset, width = todo[step]
        m = last - first
        block = group * m
        if number + 1 < len(parts):
            if piece == 0:
                held[number + 1, 0] = amplitudes[parts[number + 1][0] : parts[number + 1][1]]
                gather(number + 1, [1], step + 1)
            cut = [evens[1:][(col_size // 2 - 1) * k // pieces : (col_size // 2 - 1) * (k + 1) // pieces] for k in range(pieces)][::-1]
            gather(number + 1, cut[piece], step + 1)
            if piece:
                gather(number + 1, [q + 1 for q in cut[piece - 1]], step + 1)
        if piece == 0 and number:
            gather(number, [q + 1 for q in evens if (number, q + 1) not in held], step)
        for p in range(step):
            turn = step - 1 - p
            if 0 < turn < rounds:
                steps.post(("sum", p, turn), send(p, turn), step + 1)
            if turn == rounds and step > terms_at:
                update = write(update, p)
                steps.post("denominators", (occ_sum, vir_sum, update), step + 1)
        sources = [held[number, q] for q in range(col_size)]
        cuts = [(0, size // 2 * block), (size // 2 * block, size * block)] if size > 1 else [(0, block)]
        made[step] = product(place, sources, m, integrals, offset, width, cuts)
        steps.post(("made", step), made[step], step + 1)
        if rounds:
            steps.post(("sum", step, 0), send(step, 0), step + 2)
    for turn in range(1, rounds):
        for p in range(count):
            if ("sum", p, turn) not in held:
                held["sum", p, turn] = send(p, turn)
    for p in range(count):
        if p not in written:
            update = write(update, p)
    return update.reshape(group * own, columns)


def solution(mesh):
    placed = (P("col", "row"), P("row", "col"), P(), P(), P("row"), P("row"), P("col"), P("col"))
    return jax.shard_map(
        functools.partial(per_device, mesh.shape["row"], mesh.shape["col"]),
        mesh=mesh,
        in_specs=placed,
        out_specs=P("row", "col"),
        check_vma=False,
    )
```

```python
import functools

import jax
import jax.numpy as jnp
from jax import lax
from jax.experimental import pallas as pl
from jax.experimental.pallas import tpu as pltpu
from jax.sharding import PartitionSpec as P

PLAN = ((1, (1,)), (1, (1,)), (1, (1,)), (1, (1, 1)))
TILE_BYTES = 5500000


def lookup(table, index):
    positions = jnp.arange(table.shape[0], dtype=jnp.int32)
    picked = jnp.where(index[:, None] == positions[None, :], table[None, :], jnp.float32(0.0))
    return jnp.sum(picked, axis=1)


def halves(values):
    high = values.astype(jnp.bfloat16)
    return high, (values - high.astype(jnp.float32)).astype(jnp.bfloat16)


def product_kernel(m, sources, cuts, place_ref, *refs):
    a_refs, b_ref = refs[:sources], refs[sources]
    out_refs, stacked = refs[sources + 1 : -1], refs[-1]
    rows = stacked.shape[0] // 2

    @pl.when(pl.program_id(0) == 0)
    def _():
        q = 0
        for a_ref in a_refs:
            for at in range(0, a_ref.shape[0], m):
                high, low = halves(a_ref[at : at + m, :])
                start = pl.multiple_of(place_ref[q] * m, m)
                stacked[pl.ds(start, m), :] = high
                stacked[pl.ds(rows + start, m), :] = low
                q += 1

    b_high, b_low = halves(b_ref[...])
    both = jnp.dot(stacked[...], b_high, preferred_element_type=jnp.float32)
    total = both[:rows] + (both[rows:] + jnp.dot(stacked[:rows, :], b_low, preferred_element_type=jnp.float32))
    for out_ref, (first, last) in zip(out_refs, cuts):
        out_ref[...] = total[first:last]


def column_tile(depth, columns, offset):
    best = 128
    for tile in range(128, columns + 1, 128):
        if columns % tile == 0 and offset % tile == 0 and depth * tile * 4 <= TILE_BYTES:
            best = tile
    return best


def product(place, sources, m, integrals, offset, columns, cuts):
    depth = integrals.shape[0]
    rows = m * place.shape[0]
    tile = column_tile(depth, columns, offset)
    return pl.pallas_call(
        functools.partial(product_kernel, m, len(sources), cuts),
        grid=(columns // tile,),
        in_specs=[pl.BlockSpec(memory_space=pltpu.SMEM)]
        + [pl.BlockSpec(source.shape, lambda j: (0, 0), pipeline_mode=pl.Buffered(1)) for source in sources]
        + [pl.BlockSpec((depth, tile), lambda j: (0, j + offset // tile))],
        out_specs=[pl.BlockSpec((last - first, tile), lambda j: (0, j)) for first, last in cuts],
        out_shape=[jax.ShapeDtypeStruct((last - first, columns), jnp.float32) for first, last in cuts],
        scratch_shapes=[pltpu.VMEM((2 * rows, depth), jnp.bfloat16)],
        compiler_params=pltpu.CompilerParams(vmem_limit_bytes=58 * 2**20),
        cost_estimate=pl.CostEstimate(
            flops=6 * rows * depth * columns, bytes_accessed=4 * (depth * columns + rows * (depth + columns)), transcendentals=0
        ),
        name="ladder_product",
    )(place, *sources, integrals)


def across(block, axis, bits, size):
    return lax.ppermute(block, axis, [(i, i ^ bits) for i in range(size)])


def row_parts(own):
    if own % 16:
        return [(0, own, (1,))]
    total = sum(share for share, _ in PLAN)
    out, at, so_far = [], 0, 0
    for share, pieces in PLAN:
        so_far += share
        end = own * so_far // total // 16 * 16
        if end > at:
            out.append((at, end, pieces))
            at = end
    return out


def column_pieces(columns, pieces):
    out, at, so_far = [], 0, 0
    for share in pieces:
        so_far += share
        end = columns * so_far // sum(pieces) // 256 * 256 if so_far < sum(pieces) else columns
        if end > at:
            out.append((at, end - at))
            at = end
    return out


def plain(amplitudes, integrals):
    rows = jnp.dot(
        lax.all_gather(amplitudes, "col", axis=0, tiled=True),
        integrals,
        preferred_element_type=jnp.float32,
        precision=lax.Precision.HIGHEST,
    )
    return lax.psum_scatter(rows, "row", scatter_dimension=0, tiled=True)


class Steps:
    def __init__(self):
        self.held, self.due = {}, {}

    def post(self, key, value, step):
        self.held[key] = value
        self.due.setdefault(step, []).append(key)

    def settle(self, step, value):
        keys = self.due.pop(step, [])
        value, held = lax.optimization_barrier((value, [self.held[key] for key in keys]))
        self.held.update(zip(keys, held))
        return value


def per_device(
    size, col_size, amplitudes, integrals, occ_energy, vir_energy, occ_first, occ_second, vir_first, vir_second
):
    own, columns = amplitudes.shape[0], integrals.shape[1]
    if size & (size - 1) or col_size & (col_size - 1) or col_size % size or columns % 128 or own % 8:
        occ_sum = lookup(occ_energy, occ_first) + lookup(occ_energy, occ_second)
        vir_sum = lookup(vir_energy, vir_first) + lookup(vir_energy, vir_second)
        return plain(amplitudes, integrals) / (vir_sum[None, :] - occ_sum[:, None])
    group = col_size // size
    rounds = size.bit_length() - 1
    order = lax.axis_index("col") ^ jnp.arange(col_size, dtype=jnp.int32)
    differs, owner = lax.axis_index("row") ^ (order // group), 0
    for bit in range(rounds):
        owner = owner * 2 + (differs >> bit) % 2
    place = owner * group + order % group

    parts = row_parts(own)
    todo = []
    for number, (first, last, pieces) in enumerate(parts):
        pieces = column_pieces(columns, pieces)
        for piece, (offset, width) in enumerate(pieces):
            todo.append((number, piece, len(pieces), first, last, offset, width))
    count = len(todo)
    steps = Steps()
    held = steps.held
    evens = list(range(0, col_size, 2))

    def gather(number, wanted, due):
        for q in wanted:
            source, bits = (0, q) if q % 2 == 0 else (q - 1, 1)
            steps.post((number, q), across(held[number, source], "col", bits, col_size), due)

    def send(p, turn):
        _, _, _, first, last, _, _ = todo[p]
        block = group * (last - first)
        half = size // 2**turn // 2 * block
        if turn == 0:
            return across(made[p][1], "row", 1, size)
        values = held["sum", p, turn - 1][half:]
        kept = made[p][0][half : 2 * half]
        for earlier in range(turn - 1):
            kept = kept + held["sum", p, earlier][half : 2 * half]
        return across(values + kept, "row", 2**turn, size)

    def write(update, p):
        _, _, _, first, last, offset, width = todo[p]
        block = group * (last - first)
        ladder = made[p][0][:block]
        for turn in range(rounds):
            ladder = ladder + held["sum", p, turn][:block]
        denom = vir_sum[None, None, offset : offset + width] - occ_sum[:, first:last, None]
        return lax.dynamic_update_slice(update, ladder.reshape(group, last - first, width) / denom, (0, first, offset))

    made = {}
    held[0, 0] = amplitudes[parts[0][0] : parts[0][1]]
    gather(0, evens[1:], 0)
    if len(evens) > 1:
        held[0, evens[-1]], later = lax.optimization_barrier(
            (held[0, evens[-1]], (amplitudes, vir_first, vir_second, occ_first, occ_second))
        )
        amplitudes, vir_first, vir_second, occ_first, occ_second = later
    for number, part in enumerate(parts[1:], 1):
        steps.post((number, 0), amplitudes[part[0] : part[1]], 0)
    occ_sum = (lookup(occ_energy, occ_first) + lookup(occ_energy, occ_second)).reshape(group, own)
    vir_sum = lookup(vir_energy, vir_first) + lookup(vir_energy, vir_second)
    steps.post("terms", (occ_sum, vir_sum), 0)
    gather(0, [q + 1 for q in evens], 0)
    for step in range(count + 1):
        if step < count:
            number, piece, pieces, first, last, offset, width = todo[step]
            if number + 1 < len(parts) and step:
                steps.post((number + 1, 0), held[number + 1, 0], step)
        place = steps.settle(step, place)
        if step == count:
            break
        m = last - first
        block = group * m
        if number + 1 < len(parts):
            cut = [evens[1:][-(-(col_size // 2 - 1) * k // pieces) : -(-(col_size // 2 - 1) * (k + 1) // pieces)] for k in range(pieces)]
            gather(number + 1, cut[piece], step + 1)
            if piece:
                gather(number + 1, [q + 1 for q in ([0] if piece == 1 else []) + cut[piece - 1]], step + 1)
        if piece == 0 and number:
            gather(number, [q + 1 for q in evens if (number, q + 1) not in held], step)
        for p in range(step):
            turn = step - 1 - p
            if 0 < turn < rounds:
                steps.post(("sum", p, turn), send(p, turn), step + 1)
        sources = [held[number, q] for q in range(col_size)]
        cuts = [(0, size // 2 * block), (size // 2 * block, size * block)] if size > 1 else [(0, block)]
        made[step] = product(place, sources, m, integrals, offset, width, cuts)
        steps.post(("made", step), made[step], step + 1)
        if rounds:
            steps.post(("sum", step, 0), send(step, 0), step + 2)
    for turn in range(1, rounds):
        for p in range(count):
            if ("sum", p, turn) not in held:
                held["sum", p, turn] = send(p, turn)
    occ_sum, vir_sum = held["terms"]
    update = jnp.zeros((group, own, columns), jnp.float32)
    for p in range(count):
        update = write(update, p)
    return update.reshape(group * own, columns)


def solution(mesh):
    placed = (P("col", "row"), P("row", "col"), P(), P(), P("row"), P("row"), P("col"), P("col"))
    return jax.shard_map(
        functools.partial(per_device, mesh.shape["row"], mesh.shape["col"]),
        mesh=mesh,
        in_specs=placed,
        out_specs=P("row", "col"),
        check_vma=False,
    )
```

```python
import functools

import jax
import jax.numpy as jnp
from jax import lax
from jax.experimental import pallas as pl
from jax.experimental.pallas import tpu as pltpu
from jax.sharding import PartitionSpec as P

PLAN = ((1, (1,)), (1, (1,)), (1, (1,)), (1, (1, 1)))
TILE_BYTES = 5500000


def lookup(table, index):
    positions = jnp.arange(table.shape[0], dtype=jnp.int32)
    picked = jnp.where(index[:, None] == positions[None, :], table[None, :], jnp.float32(0.0))
    return jnp.sum(picked, axis=1)


def halves(values):
    high = values.astype(jnp.bfloat16)
    return high, (values - high.astype(jnp.float32)).astype(jnp.bfloat16)


def product_kernel(m, sources, cuts, place_ref, *refs):
    a_refs, b_ref = refs[:sources], refs[sources]
    out_refs, stacked = refs[sources + 1 : -1], refs[-1]
    rows = stacked.shape[0] // 2

    @pl.when(pl.program_id(0) == 0)
    def _():
        q = 0
        for a_ref in a_refs:
            for at in range(0, a_ref.shape[0], m):
                high, low = halves(a_ref[at : at + m, :])
                start = pl.multiple_of(place_ref[q] * m, m)
                stacked[pl.ds(start, m), :] = high
                stacked[pl.ds(rows + start, m), :] = low
                q += 1

    b_high, b_low = halves(b_ref[...])
    both = jnp.dot(stacked[...], b_high, preferred_element_type=jnp.float32)
    total = both[:rows] + (both[rows:] + jnp.dot(stacked[:rows, :], b_low, preferred_element_type=jnp.float32))
    for out_ref, (first, last) in zip(out_refs, cuts):
        out_ref[...] = total[first:last]


def column_tile(depth, columns, offset):
    best = 128
    for tile in range(128, columns + 1, 128):
        if columns % tile == 0 and offset % tile == 0 and depth * tile * 4 <= TILE_BYTES:
            best = tile
    return best


def product(place, sources, m, integrals, offset, columns, cuts):
    depth = integrals.shape[0]
    rows = m * place.shape[0]
    tile = column_tile(depth, columns, offset)
    return pl.pallas_call(
        functools.partial(product_kernel, m, len(sources), cuts),
        grid=(columns // tile,),
        in_specs=[pl.BlockSpec(memory_space=pltpu.SMEM)]
        + [pl.BlockSpec(source.shape, lambda j: (0, 0), pipeline_mode=pl.Buffered(1)) for source in sources]
        + [pl.BlockSpec((depth, tile), lambda j: (0, j + offset // tile))],
        out_specs=[pl.BlockSpec((last - first, tile), lambda j: (0, j)) for first, last in cuts],
        out_shape=[jax.ShapeDtypeStruct((last - first, columns), jnp.float32) for first, last in cuts],
        scratch_shapes=[pltpu.VMEM((2 * rows, depth), jnp.bfloat16)],
        compiler_params=pltpu.CompilerParams(vmem_limit_bytes=58 * 2**20),
        cost_estimate=pl.CostEstimate(
            flops=6 * rows * depth * columns, bytes_accessed=4 * (depth * columns + rows * (depth + columns)), transcendentals=0
        ),
        name="ladder_product",
    )(place, *sources, integrals)


def across(block, axis, bits, size):
    return lax.ppermute(block, axis, [(i, i ^ bits) for i in range(size)])


def row_parts(own):
    if own % 16:
        return [(0, own, (1,))]
    total = sum(share for share, _ in PLAN)
    out, at, so_far = [], 0, 0
    for share, pieces in PLAN:
        so_far += share
        end = own * so_far // total // 16 * 16
        if end > at:
            out.append((at, end, pieces))
            at = end
    return out


def column_pieces(columns, pieces):
    out, at, so_far = [], 0, 0
    for share in pieces:
        so_far += share
        end = columns * so_far // sum(pieces) // 256 * 256 if so_far < sum(pieces) else columns
        if end > at:
            out.append((at, end - at))
            at = end
    return out


def plain(amplitudes, integrals):
    rows = jnp.dot(
        lax.all_gather(amplitudes, "col", axis=0, tiled=True),
        integrals,
        preferred_element_type=jnp.float32,
        precision=lax.Precision.HIGHEST,
    )
    return lax.psum_scatter(rows, "row", scatter_dimension=0, tiled=True)


class Steps:
    def __init__(self):
        self.held, self.due = {}, {}

    def post(self, key, value, step):
        self.held[key] = value
        self.due.setdefault(step, []).append(key)

    def settle(self, step, value):
        keys = self.due.pop(step, [])
        value, held = lax.optimization_barrier((value, [self.held[key] for key in keys]))
        self.held.update(zip(keys, held))
        return value


def per_device(
    size, col_size, amplitudes, integrals, occ_energy, vir_energy, occ_first, occ_second, vir_first, vir_second
):
    own, columns = amplitudes.shape[0], integrals.shape[1]
    if size & (size - 1) or col_size & (col_size - 1) or col_size % size or columns % 128 or own % 8:
        occ_sum = lookup(occ_energy, occ_first) + lookup(occ_energy, occ_second)
        vir_sum = lookup(vir_energy, vir_first) + lookup(vir_energy, vir_second)
        return plain(amplitudes, integrals) / (vir_sum[None, :] - occ_sum[:, None])
    group = col_size // size
    rounds = size.bit_length() - 1
    order = lax.axis_index("col") ^ jnp.arange(col_size, dtype=jnp.int32)
    differs, owner = lax.axis_index("row") ^ (order // group), 0
    for bit in range(rounds):
        owner = owner * 2 + (differs >> bit) % 2
    place = owner * group + order % group

    parts = row_parts(own)
    todo = []
    for number, (first, last, pieces) in enumerate(parts):
        pieces = column_pieces(columns, pieces)
        for piece, (offset, width) in enumerate(pieces):
            todo.append((number, piece, len(pieces), first, last, offset, width))
    count = len(todo)
    steps = Steps()
    held = steps.held
    evens = list(range(0, col_size, 2))

    def gather(number, wanted, due):
        for q in wanted:
            source, bits = (0, q) if q % 2 == 0 else (q - 1, 1)
            steps.post((number, q), across(held[number, source], "col", bits, col_size), due)

    def send(p, turn):
        _, _, _, first, last, _, _ = todo[p]
        block = group * (last - first)
        half = size // 2**turn // 2 * block
        if turn == 0:
            return across(made[p][1], "row", 1, size)
        values = held["sum", p, turn - 1][half:]
        kept = made[p][0][half : 2 * half]
        for earlier in range(turn - 1):
            kept = kept + held["sum", p, earlier][half : 2 * half]
        return across(values + kept, "row", 2**turn, size)

    def write(update, p):
        _, _, _, first, last, offset, width = todo[p]
        block = group * (last - first)
        ladder = made[p][0][:block]
        for turn in range(rounds):
            ladder = ladder + held["sum", p, turn][:block]
        denom = vir_sum[None, None, offset : offset + width] - occ_sum[:, first:last, None]
        return lax.dynamic_update_slice(update, ladder.reshape(group, last - first, width) / denom, (0, first, offset))

    made = {}
    held[0, 0] = amplitudes[parts[0][0] : parts[0][1]]
    gather(0, evens[1:], 0)
    if len(evens) > 1:
        held[0, evens[-1]], later = lax.optimization_barrier(
            (held[0, evens[-1]], amplitudes)
        )
        amplitudes = later
    for number, part in enumerate(parts[1:], 1):
        steps.post((number, 0), amplitudes[part[0] : part[1]], 0)
    steps.post("indices", (vir_first, vir_second, occ_first, occ_second), 1)
    gather(0, [q + 1 for q in evens], 0)
    if len(parts) > 1:
        gather(1, evens[1:], 1)
    for step in range(count + 1):
        if step < count:
            number, piece, pieces, first, last, offset, width = todo[step]
            if number + 1 < len(parts) and step:
                steps.post((number + 1, 0), held[number + 1, 0], step)
        place = steps.settle(step, place)
        if step == 1:
            vir_first, vir_second, occ_first, occ_second = held["indices"]
            occ_sum = (lookup(occ_energy, occ_first) + lookup(occ_energy, occ_second)).reshape(group, own)
            vir_sum = lookup(vir_energy, vir_first) + lookup(vir_energy, vir_second)
            steps.post("terms", (occ_sum, vir_sum), 2)
        if step == count:
            break
        m = last - first
        block = group * m
        if number + 1 < len(parts):
            cut = [evens[1:][-(-(col_size // 2 - 1) * k // pieces) : -(-(col_size // 2 - 1) * (k + 1) // pieces)] for k in range(pieces)]
            if step:
                gather(number + 1, cut[piece], step + 1)
            if piece:
                gather(number + 1, [q + 1 for q in ([0] if piece == 1 else []) + cut[piece - 1]], step + 1)
        if piece == 0 and number:
            gather(number, [q + 1 for q in evens if (number, q + 1) not in held], step)
        for p in range(step):
            turn = step - 1 - p
            if 0 < turn < rounds:
                steps.post(("sum", p, turn), send(p, turn), step + 1)
        sources = [held[number, q] for q in range(col_size)]
        cuts = [(0, size // 2 * block), (size // 2 * block, size * block)] if size > 1 else [(0, block)]
        made[step] = product(place, sources, m, integrals, offset, width, cuts)
        steps.post(("made", step), made[step], step + 1)
        if rounds:
            steps.post(("sum", step, 0), send(step, 0), step + 2)
    for turn in range(1, rounds):
        for p in range(count):
            if ("sum", p, turn) not in held:
                held["sum", p, turn] = send(p, turn)
    occ_sum, vir_sum = held["terms"]
    update = jnp.zeros((group, own, columns), jnp.float32)
    for p in range(count):
        update = write(update, p)
    return update.reshape(group * own, columns)


def solution(mesh):
    placed = (P("col", "row"), P("row", "col"), P(), P(), P("row"), P("row"), P("col"), P("col"))
    return jax.shard_map(
        functools.partial(per_device, mesh.shape["row"], mesh.shape["col"]),
        mesh=mesh,
        in_specs=placed,
        out_specs=P("row", "col"),
        check_vma=False,
    )
```
